256 devices in a mesh: seq: 32 (over y, z), head: 8 (over x, core).
Axes of the slice: x: 4, y: 4, z: 8, core: 2. Of those that a mesh axis runs over, the one named last changes fastest.
Arguments:
- queries: bfloat16 [8192, 4096], P('seq', 'head'), may hold values from -140 to 140
- key_rows: bfloat16 [8192, 1024], P('seq', 'head'), may hold values from -15 to 15
- value_rows: bfloat16 [8192, 1024], P('seq', 'head'), may hold values from -4.5 to 4.5
- span_place: int32 [64], replicated, may hold values from 0 to 63, as said below
- block_lists: int32 [64, 8], replicated, may hold values from 0 to 62, as said below
- cotangent: bfloat16 [8192, 4096], P(('seq', 'head')), may hold values from -4.5 to 4.5
Outputs:
- attended: bfloat16 [8192, 4096], P(('seq', 'head'))
- query_grad: bfloat16 [8192, 4096], P('seq', 'head')
- key_grad: bfloat16 [8192, 1024], P('seq', 'head')
- value_grad: bfloat16 [8192, 1024], P('seq', 'head')
The draws below stay inside these ranges and needn't reach their ends.
Inputs may be any that keep to these rules, and one draw needn't show every extreme that they name: `span_place`: storage slots 2i and 2i+1 hold blocks c and 63 - c for some c below 32; each block is held once. `block_lists`: call blocks c and 63 - c a pair. Each entry of row b is an earlier block or b itself. Among the entries of the two rows of one pair, those that are not their own row's block lie in distinct pairs, none of them that pair.
All inputs are finite; a program needn't handle non-finite values.
Results may differ from the reference program's by a relative error of at most 0.035.
Values may be sent and summed in bfloat16 or wider, within the bound.
No kernel may reach another device: no remote copies, remote signals or barrier semaphores. Data moves between devices by JAX's collectives and lax.ppermute only.
A program may use at most 64 MiB of HBM per device.

```python
import math
import jax
import jax.numpy as jnp
from jax import lax

HEADS = 32
KV_HEADS = 8
HEAD_DIM = 128
SPAN = 128
TOPK = 8
TOKENS = 8192
N_SEQ = 32


def base_keys(key, spread):
    row_width = KV_HEADS * HEAD_DIM
    drawn_draw = jnp.clip(jax.random.normal(key, (TOKENS, row_width), jnp.float32), -4.5, 4.5)
    scale_key = jax.random.fold_in(key, 101)
    row_index = jnp.arange(TOKENS, dtype=jnp.int32)
    special = (row_index % 64 == 1) | (row_index % 64 == 2)
    row_scale = jnp.exp(spread * jax.random.uniform(scale_key, (TOKENS, 1), jnp.float32, -1.15, 1.15))
    row_scale = jnp.where(special[:, None], 1.0, row_scale)
    scaled = drawn_draw * row_scale
    target = (row_index % 64 == 1)[:, None]
    return jnp.where(target, scaled, scaled)


def draw_key_rows(key, part):
    shared = base_keys(key, 0.0)
    return shared.astype(jnp.bfloat16)


def draw_queries(key, part):
    key = jax.random.fold_in(key, 5)
    drawn_draw = jnp.clip(jax.random.normal(key, (TOKENS, HEADS * HEAD_DIM), jnp.float32), -4.5, 4.5)
    return drawn_draw.astype(jnp.bfloat16)


def draw_span_place(key, part):
    key = jax.random.fold_in(key, 7)
    order = jax.random.permutation(key, N_SEQ).astype(jnp.int32)
    return jnp.stack([order, 2 * N_SEQ - 1 - order], axis=1).reshape(-1)


def draw_block_lists(key, part):
    key = jax.random.fold_in(key, 11)
    pair_count = N_SEQ
    order_key, side_key = jax.random.split(key)
    row_keys = jax.random.split(order_key, pair_count)
    orders = jax.vmap(lambda item: jax.random.permutation(item, pair_count))(row_keys).astype(jnp.int32)
    early_block = jnp.arange(pair_count, dtype=jnp.int32)[:, None]
    position = jnp.arange(pair_count, dtype=jnp.int32)[None, :]
    first_score = position + pair_count * (orders >= early_block).astype(jnp.int32)
    first_rank = jnp.argsort(first_score, axis=1, stable=True)
    first_keys = jnp.take_along_axis(orders, first_rank[:, :TOPK], axis=1)
    first_keys = jnp.where(first_keys < early_block, first_keys, early_block)
    taken_keys = orders == early_block
    for column in range(TOPK):
        taken_keys = taken_keys | (orders == first_keys[:, column:column + 1])
    second_score = position + pair_count * taken_keys.astype(jnp.int32)
    second_rank = jnp.argsort(second_score, axis=1, stable=True)
    second_keys = jnp.take_along_axis(orders, second_rank[:, :TOPK], axis=1)
    flip_bits = jax.random.randint(side_key, (pair_count, TOPK), 0, 2)
    second_blocks = jnp.where((flip_bits == 1) & (second_keys > early_block), 2 * pair_count - 1 - second_keys, second_keys)
    return jnp.concatenate([first_keys, second_blocks[::-1]], axis=0).astype(jnp.int32)


def level_of(own_key, extent, pieces, least, top_value):
    factor_of, own = 1.0, jax.random.fold_in(own_key, 6)
    for axis_at, parts in pieces:
        steps = jnp.exp(jax.random.uniform(jax.random.fold_in(own, axis_at), (parts,), jnp.float32, least / len(pieces), top_value / len(pieces)))
        factor_of = factor_of * jnp.repeat(steps, extent[axis_at] // parts).reshape([-1 if axis == axis_at else 1 for axis in range(len(extent))])
    return factor_of


def centred(key, dims, scale, limit, shards=(), held_as=jnp.bfloat16):
    entries = scale * jax.random.normal(key, dims, jnp.float32)
    if shards:
        entries = entries * level_of(key, dims, shards, -0.22, 0.18)
    return jnp.clip(entries, -limit, limit).astype(held_as)


def setup_inputs(seed: int = 0) -> dict:
    key_list = jax.random.split(jax.random.key(seed), 7)
    return {
        "queries": draw_queries(jax.random.fold_in(key_list[6], 71), 0),
        "key_rows": draw_key_rows(jax.random.fold_in(key_list[6], 71), 0),
        "value_rows": centred(key_list[2], (TOKENS, KV_HEADS * HEAD_DIM), 1.0, 4.5, ((0, 32), (1, 8))),
        "span_place": draw_span_place(jax.random.fold_in(key_list[6], 71), 0),
        "block_lists": draw_block_lists(jax.random.fold_in(key_list[6], 71), 0),
        "cotangent": centred(key_list[5], (TOKENS, HEADS * HEAD_DIM), 1.0, 4.5, ((0, 256),)),
    }


def lookup(lookup_table, selector, table_rows):
    matches = selector[..., None] == jnp.arange(table_rows, dtype=jnp.int32)
    return lax.optimization_barrier(jnp.sum(jnp.where(matches[..., None], lookup_table, 0), axis=-2))

def block_layout(span_place, block_lists):
    slot_total = span_place.shape[0]
    slot_ids = jnp.arange(slot_total, dtype=jnp.int32)
    slot_of = lax.optimization_barrier(jnp.sum(jnp.where(span_place[:, None] == slot_ids[None, :], slot_ids[:, None], 0), axis=0))
    pick_blocks = lookup(block_lists, span_place, slot_total)
    valid_cols = []
    for column in range(pick_blocks.shape[1]):
        kept_pick = pick_blocks[:, column] != span_place
        for before in range(column):
            kept_pick = kept_pick & (pick_blocks[:, column] != pick_blocks[:, before])
        valid_cols.append(kept_pick)
    pick_valid = jnp.stack(valid_cols, axis=1)
    pick_slots = lookup(slot_of[:, None], pick_blocks, slot_total)[..., 0]
    return (pick_slots.astype(jnp.int32), pick_valid)

def attend_block(query_block, key_set, value_set, grad_block, visible_picks, score_scale):
    span_rows = query_block.shape[0]
    set_count = key_set.shape[0]
    query_wide = query_block.astype(jnp.float32)
    keys_wide = key_set.astype(jnp.float32)
    values_wide = value_set.astype(jnp.float32)
    grad_wide = grad_block.astype(jnp.float32)
    scores = jnp.einsum('ckgd,jekd->kgcje', query_wide, keys_wide) * score_scale
    causal = jnp.arange(span_rows)[None, :] <= jnp.arange(span_rows)[:, None]
    others = jnp.broadcast_to(visible_picks[None, :, None], (span_rows, set_count - 1, span_rows))
    allowed = jnp.concatenate([causal[:, None, :], others], axis=1)
    scores = jnp.where(allowed, scores, -jnp.inf)
    row_top = lax.optimization_barrier(jnp.max(scores, axis=(3, 4), keepdims=True))
    row_total = lax.optimization_barrier(jnp.sum(jnp.exp(scores - row_top), axis=(3, 4), keepdims=True))
    log_total = row_top + jnp.log(row_total)
    probabilities = jnp.exp(scores - log_total)
    weights = lax.optimization_barrier(probabilities.astype(jnp.bfloat16)).astype(jnp.float32)
    attended = jnp.einsum('kgcje,jekd->ckgd', weights, values_wide).astype(jnp.bfloat16)
    attended_wide = lax.optimization_barrier(attended).astype(jnp.float32)
    row_delta = lax.optimization_barrier(jnp.sum(grad_wide * attended_wide, axis=-1))
    slopes = jnp.einsum('ckgd,jekd->kgcje', grad_wide, values_wide)
    shifted = slopes - jnp.transpose(row_delta, (1, 2, 0))[..., None, None]
    dscores = (probabilities * shifted * score_scale).astype(jnp.bfloat16)
    dscores_wide = lax.optimization_barrier(dscores).astype(jnp.float32)
    query_grad = jnp.einsum('kgcje,jekd->ckgd', dscores_wide, keys_wide).astype(jnp.bfloat16)
    key_part = jnp.einsum('kgcje,ckgd->jekd', dscores_wide, query_wide)
    value_part = jnp.einsum('kgcje,ckgd->jekd', weights, grad_wide)
    return (attended, query_grad, key_part, value_part)

def reference(queries, key_rows, value_rows, span_place, block_lists, cotangent):
    slot_total = 2 * N_SEQ
    group_size = HEADS // KV_HEADS
    score_scale = 1.0 / math.sqrt(HEAD_DIM)
    pick_slots, pick_valid = block_layout(span_place, block_lists)
    query_blocks = queries.reshape(slot_total, SPAN, KV_HEADS, group_size, HEAD_DIM)
    key_blocks = key_rows.reshape(slot_total, SPAN, KV_HEADS, HEAD_DIM)
    value_blocks = value_rows.reshape(slot_total, SPAN, KV_HEADS, HEAD_DIM)
    grad_blocks = cotangent.reshape(slot_total, SPAN, KV_HEADS, group_size, HEAD_DIM)

    def slot_step(held_grads, slot_id):
        key_sum, value_sum = held_grads
        sources = jnp.concatenate([slot_id[None], pick_slots[slot_id]]).astype(jnp.int32)
        attended, query_grad, key_part, value_part = attend_block(query_blocks[slot_id], key_blocks[sources], value_blocks[sources], grad_blocks[slot_id], pick_valid[slot_id], score_scale)
        key_round, value_round = lax.optimization_barrier((key_part[1:].astype(jnp.bfloat16), value_part[1:].astype(jnp.bfloat16)))
        targets = pick_slots[slot_id]
        key_sum = key_sum.at[slot_id].add(key_part[0]).at[targets].add(key_round.astype(jnp.float32))
        value_sum = value_sum.at[slot_id].add(value_part[0]).at[targets].add(value_round.astype(jnp.float32))
        return ((key_sum, value_sum), (attended, query_grad))
    zero_grad = jnp.zeros((slot_total, SPAN, KV_HEADS, HEAD_DIM), jnp.float32)
    (key_sum, value_sum), (attended, query_grad) = lax.scan(slot_step, (zero_grad, zero_grad), jnp.arange(slot_total, dtype=jnp.int32))
    return (attended.reshape(TOKENS, HEADS * HEAD_DIM), query_grad.reshape(TOKENS, HEADS * HEAD_DIM), key_sum.astype(jnp.bfloat16).reshape(TOKENS, KV_HEADS * HEAD_DIM), value_sum.astype(jnp.bfloat16).reshape(TOKENS, KV_HEADS * HEAD_DIM))
```

```python
import math

import jax
import jax.numpy as jnp
from jax import lax
from jax.experimental import pallas as pl
from jax.experimental.pallas import tpu as pltpu
from jax.sharding import PartitionSpec as P

HEAD_DIM = 128
SPAN = 128
HIDDEN = -1.0e30
SMEM = pl.BlockSpec(memory_space=pltpu.SMEM)
VMEM = pl.BlockSpec(memory_space=pltpu.VMEM)
NT = (((1,), (1,)), ((), ()))
TN = (((0,), (0,)), ((), ()))


def params(mib=40):
    return pltpu.CompilerParams(vmem_limit_bytes=mib * 1024 * 1024)


def pack_kernel(me_ref, place_ref, lists_ref, key_ref, value_ref, packed_ref, serve_ref, picks_ref, slot_of):
    pairs = packed_ref.shape[0]
    picked = lists_ref.shape[1]
    me = me_ref[0]
    first, second = place_ref[2 * me], place_ref[2 * me + 1]

    @pl.loop(0, 2 * pairs)
    def _(slot):
        slot_of[place_ref[slot]] = slot

    for side in range(2):
        block = place_ref[2 * me + side]
        for j in range(picked):
            pick = lists_ref[block, j]
            picks_ref[side * picked + j] = jnp.where(pick == block, -1, slot_of[pick] // 2)

    @pl.loop(0, pairs)
    def _(other):
        half = jnp.int32(-1)
        for side in range(2):
            block = place_ref[2 * other + side]
            for j in range(picked):
                pick = lists_ref[block, j]
                half = jnp.where(pick == first, 0, half)
                half = jnp.where(pick == second, 1, half)
        half = jnp.where(other == me, -1, half)
        serve_ref[other] = half
        start = pl.multiple_of(jnp.maximum(half, 0) * SPAN, SPAN)
        packed_ref[other, :, :HEAD_DIM] = key_ref[pl.ds(start, SPAN), :]
        packed_ref[other, :, HEAD_DIM:] = value_ref[pl.ds(start, SPAN), :]


def attend_kernel(
    picks_ref, q_ref, g_ref, k_ref, v_ref, got_ref, out_ref, dq_ref, own_ref, sent_ref,
    keys, values, scores, weights, slopes,
):
    slot = pl.program_id(0)
    picked = picks_ref.shape[0] // 2
    heads = q_ref.shape[1] // HEAD_DIM
    scale = 1.0 / math.sqrt(HEAD_DIM)
    owners = [picks_ref[slot * picked + j] for j in range(picked)]
    keys[:SPAN] = k_ref[...]
    values[:SPAN] = v_ref[...]
    for j, owner in enumerate(owners):
        rows = pl.ds((j + 1) * SPAN, SPAN)
        at = jnp.maximum(owner, 0)
        keys[rows, :] = got_ref[at, :, :HEAD_DIM]
        values[rows, :] = got_ref[at, :, HEAD_DIM:]
    columns = [slice(h * HEAD_DIM, (h + 1) * HEAD_DIM) for h in range(heads)]
    q = jnp.concatenate([q_ref[:, c] for c in columns], axis=0)
    g = jnp.concatenate([g_ref[:, c] for c in columns], axis=0)
    rows_all = heads * SPAN
    top = None
    for j in range(picked + 1):
        rows = pl.ds(j * SPAN, SPAN)
        part = lax.dot_general(keys[rows, :], q, NT, preferred_element_type=jnp.float32)
        part = part * (scale * math.log2(math.e))
        if j == 0:
            key_at = lax.broadcasted_iota(jnp.int32, (SPAN, rows_all), 0)
            query_at = lax.broadcasted_iota(jnp.int32, (SPAN, rows_all), 1) % SPAN
            part = jnp.where(key_at <= query_at, part, HIDDEN)
        else:
            part = jnp.where(owners[j - 1] >= 0, part, HIDDEN)
        scores[rows, :] = part
        here = jnp.max(part, axis=0, keepdims=True)
        top = here if top is None else jnp.maximum(top, here)
    total = jnp.zeros_like(top)
    for j in range(picked + 1):
        rows = pl.ds(j * SPAN, SPAN)
        part = jnp.exp2(scores[rows, :] - top)
        scores[rows, :] = part
        total = total + jnp.sum(part, axis=0, keepdims=True)
    inverse = 1.0 / total
    for j in range(picked + 1):
        rows = pl.ds(j * SPAN, SPAN)
        weights[rows, :] = (scores[rows, :] * inverse).astype(jnp.bfloat16)
    out_t = lax.dot_general(values[...], weights[...], TN, preferred_element_type=jnp.float32)
    out_t = out_t.astype(jnp.bfloat16).astype(jnp.float32)
    out = out_t.T.astype(jnp.bfloat16)
    for h, c in enumerate(columns):
        out_ref[:, c] = out[h * SPAN:(h + 1) * SPAN, :]
    delta = jnp.sum(g.astype(jnp.float32).T * out_t, axis=0, keepdims=True)
    inverse = inverse * scale
    for j in range(picked + 1):
        rows = pl.ds(j * SPAN, SPAN)
        part = lax.dot_general(values[rows, :], g, NT, preferred_element_type=jnp.float32)
        slopes[rows, :] = (scores[rows, :] * inverse * (part - delta)).astype(jnp.bfloat16)
    dq_t = lax.dot_general(keys[...], slopes[...], TN, preferred_element_type=jnp.float32)
    dq = dq_t.T.astype(jnp.bfloat16)
    for h, c in enumerate(columns):
        dq_ref[:, c] = dq[h * SPAN:(h + 1) * SPAN, :]
    key_part = jnp.dot(slopes[...], q, preferred_element_type=jnp.float32)
    value_part = jnp.dot(weights[...], g, preferred_element_type=jnp.float32)
    own_ref[:, :HEAD_DIM] = key_part[:SPAN]
    own_ref[:, HEAD_DIM:] = value_part[:SPAN]
    for j, owner in enumerate(owners):
        @pl.when(owner >= 0)
        def _():
            rows = slice((j + 1) * SPAN, (j + 2) * SPAN)
            sent_ref[owner, :, :HEAD_DIM] = key_part[rows].astype(jnp.bfloat16)
            sent_ref[owner, :, HEAD_DIM:] = value_part[rows].astype(jnp.bfloat16)


def add_kernel(serve_ref, own_ref, back_ref, dk_ref, dv_ref, total):
    total[...] = own_ref[...]

    @pl.loop(0, back_ref.shape[0])
    def _(other):
        half = serve_ref[other]

        @pl.when(half >= 0)
        def _():
            start = pl.multiple_of(half * SPAN, SPAN)
            total[pl.ds(start, SPAN), :] += back_ref[other].astype(jnp.float32)

    dk_ref[...] = total[:, :HEAD_DIM].astype(jnp.bfloat16)
    dv_ref[...] = total[:, HEAD_DIM:].astype(jnp.bfloat16)


def body(queries, key_rows, value_rows, span_place, block_lists, cotangent):
    pairs = lax.axis_size("seq")
    picked = block_lists.shape[1]
    width = queries.shape[1]
    bf16 = jnp.bfloat16
    me = lax.axis_index("seq").astype(jnp.int32)[None]
    moved = jax.ShapeDtypeStruct((pairs, SPAN, 2 * HEAD_DIM), bf16)
    packed, serve, picks = pl.pallas_call(
        pack_kernel,
        out_shape=(
            moved,
            jax.ShapeDtypeStruct((pairs,), jnp.int32),
            jax.ShapeDtypeStruct((2 * picked,), jnp.int32),
        ),
        in_specs=[SMEM, SMEM, SMEM, VMEM, VMEM],
        out_specs=(VMEM, SMEM, SMEM),
        scratch_shapes=[pltpu.SMEM((2 * pairs,), jnp.int32)],
        compiler_params=params(),
        name="pack",
    )(me, span_place, block_lists, key_rows, value_rows)
    got = lax.all_to_all(packed, "seq", split_axis=0, concat_axis=0, tiled=True)
    grad_heads = lax.all_to_all(cotangent, "head", split_axis=1, concat_axis=0, tiled=True)
    rows_all = (picked + 1) * SPAN
    half_wide = pl.BlockSpec((SPAN, width), lambda i: (i, 0))
    half_head = pl.BlockSpec((SPAN, HEAD_DIM), lambda i: (i, 0))
    whole = pl.BlockSpec(moved.shape, lambda i: (0, 0, 0))
    attended, query_grad, own, sent = pl.pallas_call(
        attend_kernel,
        grid=(2,),
        out_shape=(
            jax.ShapeDtypeStruct(queries.shape, bf16),
            jax.ShapeDtypeStruct(queries.shape, bf16),
            jax.ShapeDtypeStruct((2 * SPAN, 2 * HEAD_DIM), jnp.float32),
            moved,
        ),
        in_specs=[SMEM, half_wide, half_wide, half_head, half_head, whole],
        out_specs=(half_wide, half_wide, pl.BlockSpec((SPAN, 2 * HEAD_DIM), lambda i: (i, 0)), whole),
        scratch_shapes=[
            pltpu.VMEM((rows_all, HEAD_DIM), bf16),
            pltpu.VMEM((rows_all, HEAD_DIM), bf16),
            pltpu.VMEM((rows_all, width), jnp.float32),
            pltpu.VMEM((rows_all, width), bf16),
            pltpu.VMEM((rows_all, width), bf16),
        ],
        compiler_params=params(),
        name="attend",
    )(picks, queries, grad_heads, key_rows, value_rows, got)
    back = lax.all_to_all(sent, "seq", split_axis=0, concat_axis=0, tiled=True)
    attended_out = lax.all_to_all(attended, "head", split_axis=0, concat_axis=1, tiled=True)
    key_grad, value_grad = pl.pallas_call(
        add_kernel,
        out_shape=(
            jax.ShapeDtypeStruct(key_rows.shape, bf16),
            jax.ShapeDtypeStruct(value_rows.shape, bf16),
        ),
        in_specs=[SMEM, VMEM, VMEM],
        out_specs=(VMEM, VMEM),
        scratch_shapes=[pltpu.VMEM((2 * SPAN, 2 * HEAD_DIM), jnp.float32)],
        compiler_params=params(),
        name="add",
    )(serve, own, back)
    return (attended_out, query_grad, key_grad, value_grad)


def solution(mesh):
    in_specs = (
        P("seq", "head"),
        P("seq", "head"),
        P("seq", "head"),
        P(),
        P(),
        P(("seq", "head"), None),
    )
    out_specs = (P(("seq", "head"), None), P("seq", "head"), P("seq", "head"), P("seq", "head"))
    return jax.shard_map(body, mesh=mesh, in_specs=in_specs, out_specs=out_specs, check_vma=False)
```

```python
import math

import jax
import jax.numpy as jnp
from jax import lax
from jax.experimental import pallas as pl
from jax.experimental.pallas import tpu as pltpu
from jax.sharding import PartitionSpec as P

HEAD_DIM = 128
SPAN = 128
RING = 8
HIDDEN = -1.0e30
SCALE = 1.0 / math.sqrt(HEAD_DIM)
SMEM = pl.BlockSpec(memory_space=pltpu.SMEM)
VMEM = pl.BlockSpec(memory_space=pltpu.VMEM)
ANY = pl.BlockSpec(memory_space=pl.ANY)
NT = (((1,), (1,)), ((), ()))
TN = (((0,), (0,)), ((), ()))
bf16 = jnp.bfloat16
f32 = jnp.float32


def params(mib=40):
    return pltpu.CompilerParams(vmem_limit_bytes=mib * 1024 * 1024)


def route_kernel(me_ref, place_ref, lists_ref, picks_ref, table_ref, slot_of):
    pairs = place_ref.shape[0] // 2
    picked = lists_ref.shape[1]
    lines = pairs // RING
    me = me_ref[0]
    for slot in range(2 * pairs):
        slot_of[place_ref[slot]] = slot
    for at in range(lines * pairs):
        table_ref[at] = -1
    marks = []
    for line in range(lines):
        other = line * RING + me % RING
        for side in range(2):
            block = place_ref[2 * other + side]
            for j in range(picked):
                pick = lists_ref[block, j]
                slot = slot_of[pick]
                marks.append((jnp.where(pick == block, lines * pairs, line * pairs + slot // 2), slot % 2))
    own = []
    for side in range(2):
        block = place_ref[2 * me + side]
        for j in range(picked):
            pick = lists_ref[block, j]
            own.append(jnp.where(pick == block, -1, slot_of[pick] // 2))
    for at, half in marks:
        table_ref[at] = half
    for at, owner in enumerate(own):
        picks_ref[at] = owner


def columns_kernel(cot_ref, after_ref, cols_ref):
    wide = cols_ref.shape[2]
    for part in range(cols_ref.shape[0]):
        cols_ref[part] = cot_ref[:, part * wide:(part + 1) * wide]


def line_kernel(me_ref, table_ref, *refs):
    blocks, outs = refs[:RING], refs[RING:]
    lines = len(outs)
    pairs = lines * RING
    me = me_ref[0]
    mine, at = me // RING, me % RING
    for shift, block in enumerate(blocks):
        source = (at + shift) % RING
        for step, out in enumerate(outs):
            half = table_ref[(mine + step) % lines * pairs + mine * RING + source]
            out[source] = block[pl.ds(pl.multiple_of(jnp.maximum(half, 0) * SPAN, SPAN), SPAN), :]


def stack_heads(ref):
    return jnp.concatenate(
        [ref[:, h * HEAD_DIM:(h + 1) * HEAD_DIM] for h in range(ref.shape[1] // HEAD_DIM)], axis=0
    )


def store_heads(ref, transposed):
    rows = transposed.T.astype(bf16)
    for h in range(ref.shape[1] // HEAD_DIM):
        ref[:, h * HEAD_DIM:(h + 1) * HEAD_DIM] = rows[h * SPAN:(h + 1) * SPAN, :]


def attend_kernel(me_ref, picks_ref, q_ref, g_ref, k_ref, v_ref, *refs):
    lines = (len(refs) - 10) // 2
    got, (out_ref, dq_ref, ownk_ref, ownv_ref), sent = refs[:lines], refs[lines:lines + 4], refs[lines + 4:-6]
    pool, keys, values, scores, weights, slopes = refs[-6:]
    slot = pl.program_id(0)
    mine = me_ref[0] // RING
    picked = picks_ref.shape[0] // 2
    owners = [picks_ref[slot * picked + j] for j in range(picked)]

    @pl.when(slot == 0)
    def _():
        for far, ref in enumerate(got):
            pool[far] = ref[...]

    keys[:SPAN] = k_ref[...]
    values[:SPAN] = v_ref[...]
    for j, owner in enumerate(owners):
        owner = jnp.maximum(owner, 0)
        far = (mine - owner // RING + lines) % lines
        keys[(j + 1) * SPAN:(j + 2) * SPAN, :] = pool[far, owner % RING, :, :HEAD_DIM]
        values[(j + 1) * SPAN:(j + 2) * SPAN, :] = pool[far, owner % RING, :, HEAD_DIM:]
    q = stack_heads(q_ref)
    across = q.shape[0]
    top = None
    for j in range(picked + 1):
        rows = pl.ds(j * SPAN, SPAN)
        part = lax.dot_general(keys[rows, :], q, NT, preferred_element_type=f32)
        part = part * (SCALE * math.log2(math.e))
        if j == 0:
            key_at = lax.broadcasted_iota(jnp.int32, (SPAN, across), 0)
            query_at = lax.broadcasted_iota(jnp.int32, (SPAN, across), 1) % SPAN
            part = jnp.where(key_at <= query_at, part, HIDDEN)
        else:
            part = jnp.where(owners[j - 1] >= 0, part, HIDDEN)
        scores[rows, :] = part
        here = jnp.max(part, axis=0, keepdims=True)
        top = here if top is None else jnp.maximum(top, here)
    total = jnp.zeros_like(top)
    for j in range(picked + 1):
        rows = pl.ds(j * SPAN, SPAN)
        part = jnp.exp2(scores[rows, :] - top)
        scores[rows, :] = part
        total = total + jnp.sum(part, axis=0, keepdims=True)
    inverse = 1.0 / total
    for j in range(picked + 1):
        rows = pl.ds(j * SPAN, SPAN)
        weights[rows, :] = (scores[rows, :] * inverse).astype(bf16)
    g = stack_heads(g_ref)
    out_t = lax.dot_general(values[...], weights[...], TN, preferred_element_type=f32)
    out_t = out_t.astype(bf16).astype(f32)
    store_heads(out_ref, out_t)
    delta = jnp.sum(g.astype(f32).T * out_t, axis=0, keepdims=True)
    inverse = inverse * SCALE
    for j in range(picked + 1):
        rows = pl.ds(j * SPAN, SPAN)
        part = lax.dot_general(values[rows, :], g, NT, preferred_element_type=f32)
        slopes[rows, :] = (scores[rows, :] * inverse * (part - delta)).astype(bf16)
    store_heads(dq_ref, lax.dot_general(keys[...], slopes[...], TN, preferred_element_type=f32))
    key_part = jnp.dot(slopes[...], q, preferred_element_type=f32)
    value_part = jnp.dot(weights[...], g, preferred_element_type=f32)
    ownk_ref[...] = key_part[:SPAN]
    ownv_ref[...] = value_part[:SPAN]
    for j, owner in enumerate(owners):
        step = (jnp.maximum(owner, 0) // RING - mine + lines) % lines
        rows = slice((j + 1) * SPAN, (j + 2) * SPAN)
        for far in range(lines):
            @pl.when((owner >= 0) & (step == far))
            def _():
                sent[far][owner % RING, :, :HEAD_DIM] = key_part[rows].astype(bf16)
                sent[far][owner % RING, :, HEAD_DIM:] = value_part[rows].astype(bf16)


def line_sum_kernel(me_ref, table_ref, after_ref, *refs):
    backs, outs = refs[:-RING], refs[-RING:]
    lines = len(backs)
    pairs = lines * RING
    me = me_ref[0]
    mine, at = me // RING, me % RING
    for shift, out in enumerate(outs):
        owner = (at + shift) % RING
        halves = [
            table_ref[(mine - step + lines) % lines * pairs + mine * RING + owner] for step in range(lines)
        ]
        parts = [back[owner].astype(f32) for back in backs]
        for side in range(2):
            total = jnp.zeros((SPAN, 2 * HEAD_DIM), f32)
            for half, part in zip(halves, parts):
                total += jnp.where(half == side, part, 0.0)
            out[side * SPAN:(side + 1) * SPAN, :] = total.astype(bf16)


def add_kernel(ownk_ref, ownv_ref, *refs):
    parts, outs = refs[:RING], refs[RING:]
    for which, (own, out) in enumerate(zip((ownk_ref, ownv_ref), outs)):
        total = own[...]
        for part in parts:
            total += part[:, which * HEAD_DIM:(which + 1) * HEAD_DIM].astype(f32)
        out[...] = total.astype(bf16)


def body(queries, key_rows, value_rows, span_place, block_lists, cotangent):
    pairs = lax.axis_size("seq")
    lines = pairs // RING
    head_count = lax.axis_size("head")
    picked = block_lists.shape[1]
    width = queries.shape[1]
    me = lax.axis_index("seq").astype(jnp.int32)[None]
    shape = jax.ShapeDtypeStruct
    lined = shape((RING, SPAN, 2 * HEAD_DIM), bf16)
    both = shape((2 * SPAN, 2 * HEAD_DIM), bf16)

    def shift(array, y_step, z_step):
        moves = [
            (y * RING + z, (y + y_step) % lines * RING + (z + z_step) % RING)
            for y in range(lines)
            for z in range(RING)
        ]
        return lax.ppermute(array, "seq", moves)

    def over_lines(parts):
        got = list(parts)
        for step in (1, lines - 1, *range(2, lines - 1)):
            got[step] = shift(parts[step], step, 0)
        return got

    own = jnp.concatenate([key_rows, value_rows], axis=1)
    below, above = [own], [own]
    for _ in range(RING // 2 - 1):
        below.append(shift(below[-1], 0, 1))
        above.append(shift(above[-1], 0, -1))
    above.append(shift(above[-1], 0, -1))
    picks, table = pl.pallas_call(
        route_kernel,
        out_shape=(shape((2 * picked,), jnp.int32), shape((lines * pairs + 1,), jnp.int32)),
        in_specs=[SMEM, SMEM, SMEM],
        out_specs=(SMEM, SMEM),
        scratch_shapes=[pltpu.SMEM((2 * pairs,), jnp.int32)],
        compiler_params=params(),
        name="route",
    )(me, span_place, block_lists)
    lined_out = pl.pallas_call(
        line_kernel,
        out_shape=[lined] * lines,
        in_specs=[SMEM, SMEM] + [VMEM] * RING,
        out_specs=[VMEM] * lines,
        compiler_params=params(),
        name="line",
    )(me, table, *above, *below[:0:-1])
    got = over_lines(lined_out)
    columns = pl.pallas_call(
        columns_kernel,
        out_shape=shape((head_count, cotangent.shape[0], width), bf16),
        in_specs=[VMEM, ANY],
        out_specs=VMEM,
        compiler_params=params(),
        name="columns",
    )(cotangent, lined_out[0])
    grad_heads = lax.all_to_all(columns, "head", split_axis=0, concat_axis=0, tiled=True)
    grad_heads = grad_heads.reshape(queries.shape)

    rows_all = (picked + 1) * SPAN
    half_wide = pl.BlockSpec((SPAN, width), lambda i: (i, 0))
    half_head = pl.BlockSpec((SPAN, HEAD_DIM), lambda i: (i, 0))
    eighth = pl.BlockSpec(lined.shape, lambda i: (0, 0, 0))
    attended, query_grad, own_keys, own_values, *sent = pl.pallas_call(
        attend_kernel,
        grid=(2,),
        out_shape=[
            shape(queries.shape, bf16),
            shape(queries.shape, bf16),
            shape(key_rows.shape, f32),
            shape(key_rows.shape, f32),
        ] + [lined] * lines,
        in_specs=[SMEM, SMEM, half_wide, half_wide, half_head, half_head] + [eighth] * lines,
        out_specs=[half_wide, half_wide, half_head, half_head] + [eighth] * lines,
        scratch_shapes=[
            pltpu.VMEM((lines, *lined.shape), bf16),
            pltpu.VMEM((rows_all, HEAD_DIM), bf16),
            pltpu.VMEM((rows_all, HEAD_DIM), bf16),
            pltpu.VMEM((rows_all, width), f32),
            pltpu.VMEM((rows_all, width), bf16),
            pltpu.VMEM((rows_all, width), bf16),
        ],
        compiler_params=params(),
        name="attend",
    )(me, picks, queries, grad_heads, key_rows, value_rows, *got)

    back_line = over_lines(sent)
    attended_out = lax.all_to_all(attended, "head", split_axis=0, concat_axis=1, tiled=True)
    line_sums = pl.pallas_call(
        line_sum_kernel,
        out_shape=[both] * RING,
        in_specs=[SMEM, SMEM, ANY] + [VMEM] * lines,
        out_specs=[VMEM] * RING,
        compiler_params=params(),
        name="line_sum",
    )(me, table, attended_out, *back_line)
    back = [line_sums[0]]
    for far in (*(step for near in range(1, RING // 2) for step in (near, RING - near)), RING // 2):
        back.append(shift(line_sums[far], 0, far))
    key_grad, value_grad = pl.pallas_call(
        add_kernel,
        out_shape=(shape(key_rows.shape, bf16), shape(value_rows.shape, bf16)),
        in_specs=[VMEM] * (2 + RING),
        out_specs=(VMEM, VMEM),
        compiler_params=params(),
        name="add",
    )(own_keys, own_values, *back)
    return (attended_out, query_grad, key_grad, value_grad)


def solution(mesh):
    in_specs = (
        P("seq", "head"),
        P("seq", "head"),
        P("seq", "head"),
        P(),
        P(),
        P(("seq", "head"), None),
    )
    out_specs = (P(("seq", "head"), None), P("seq", "head"), P("seq", "head"), P("seq", "head"))
    return jax.shard_map(body, mesh=mesh, in_specs=in_specs, out_specs=out_specs, check_vma=False)
```

```python
import functools
import math

import jax
import jax.numpy as jnp
from jax import lax
from jax.experimental import pallas as pl
from jax.experimental.pallas import tpu as pltpu
from jax.sharding import PartitionSpec as P

HEAD_DIM = 128
SPAN = 128
RING = 8
HIDDEN = -1.0e30
GROUPS = ((3, 5, 2, 6), (4, 1, 7, 0))
SCALE = 1.0 / math.sqrt(HEAD_DIM)
SMEM = pl.BlockSpec(memory_space=pltpu.SMEM)
VMEM = pl.BlockSpec(memory_space=pltpu.VMEM)
ANY = pl.BlockSpec(memory_space=pl.ANY)
NT = (((1,), (1,)), ((), ()))
TN = (((0,), (0,)), ((), ()))
bf16 = jnp.bfloat16
f32 = jnp.float32


def params(mib=40):
    return pltpu.CompilerParams(vmem_limit_bytes=mib * 1024 * 1024)


def route_kernel(me_ref, place_ref, lists_ref, picks_ref, table_ref, slot_of):
    pairs = place_ref.shape[0] // 2
    picked = lists_ref.shape[1]
    lines = pairs // RING
    me = me_ref[0]
    for slot in range(2 * pairs):
        slot_of[place_ref[slot]] = slot
    for at in range(lines * pairs):
        table_ref[at] = -1
    marks = []
    for line in range(lines):
        other = line * RING + me % RING
        for side in range(2):
            block = place_ref[2 * other + side]
            for j in range(picked):
                pick = lists_ref[block, j]
                slot = slot_of[pick]
                marks.append((jnp.where(pick == block, lines * pairs, line * pairs + slot // 2), slot % 2))
    own = []
    for side in range(2):
        block = place_ref[2 * me + side]
        for j in range(picked):
            pick = lists_ref[block, j]
            own.append(jnp.where(pick == block, -1, slot_of[pick] // 2))
    for at, half in marks:
        table_ref[at] = half
    for at, owner in enumerate(own):
        picks_ref[at] = owner


def columns_kernel(cot_ref, after_ref, cols_ref):
    wide = cols_ref.shape[2]
    for part in range(cols_ref.shape[0]):
        cols_ref[part] = cot_ref[:, part * wide:(part + 1) * wide]


def line_kernel(me_ref, table_ref, *refs):
    blocks, outs = refs[:RING], refs[RING:]
    lines = len(outs)
    pairs = lines * RING
    me = me_ref[0]
    mine, at = me // RING, me % RING
    for shift, block in enumerate(blocks):
        source = (at + shift) % RING
        for step, out in enumerate(outs):
            half = table_ref[(mine + step) % lines * pairs + mine * RING + source]
            out[source] = block[pl.ds(pl.multiple_of(jnp.maximum(half, 0) * SPAN, SPAN), SPAN), :]


def stack_heads(ref):
    return jnp.concatenate(
        [ref[:, h * HEAD_DIM:(h + 1) * HEAD_DIM] for h in range(ref.shape[1] // HEAD_DIM)], axis=0
    )


def store_heads(ref, transposed):
    rows = transposed.T.astype(bf16)
    for h in range(ref.shape[1] // HEAD_DIM):
        ref[:, h * HEAD_DIM:(h + 1) * HEAD_DIM] = rows[h * SPAN:(h + 1) * SPAN, :]


def attend_kernel(me_ref, picks_ref, q_ref, g_ref, k_ref, v_ref, *refs):
    lines = (len(refs) - 10) // (1 + len(GROUPS))
    got, (out_ref, dq_ref, ownk_ref, ownv_ref), sent = refs[:lines], refs[lines:lines + 4], refs[lines + 4:-6]
    pool, keys, values, scores, weights, slopes = refs[-6:]
    slot = pl.program_id(0)
    mine, at = me_ref[0] // RING, me_ref[0] % RING
    picked = picks_ref.shape[0] // 2
    owners = [picks_ref[slot * picked + j] for j in range(picked)]

    @pl.when(slot == 0)
    def _():
        for far, ref in enumerate(got):
            pool[far] = ref[...]

    keys[:SPAN] = k_ref[...]
    values[:SPAN] = v_ref[...]
    for j, owner in enumerate(owners):
        owner = jnp.maximum(owner, 0)
        far = (mine - owner // RING + lines) % lines
        keys[(j + 1) * SPAN:(j + 2) * SPAN, :] = pool[far, owner % RING, :, :HEAD_DIM]
        values[(j + 1) * SPAN:(j + 2) * SPAN, :] = pool[far, owner % RING, :, HEAD_DIM:]
    q = stack_heads(q_ref)
    across = q.shape[0]
    top = None
    for j in range(picked + 1):
        rows = pl.ds(j * SPAN, SPAN)
        part = lax.dot_general(keys[rows, :], q, NT, preferred_element_type=f32)
        part = part * (SCALE * math.log2(math.e))
        if j == 0:
            key_at = lax.broadcasted_iota(jnp.int32, (SPAN, across), 0)
            query_at = lax.broadcasted_iota(jnp.int32, (SPAN, across), 1) % SPAN
            part = jnp.where(key_at <= query_at, part, HIDDEN)
        else:
            part = jnp.where(owners[j - 1] >= 0, part, HIDDEN)
        scores[rows, :] = part
        here = jnp.max(part, axis=0, keepdims=True)
        top = here if top is None else jnp.maximum(top, here)
    total = jnp.zeros_like(top)
    for j in range(picked + 1):
        rows = pl.ds(j * SPAN, SPAN)
        part = jnp.exp2(scores[rows, :] - top)
        scores[rows, :] = part
        total = total + jnp.sum(part, axis=0, keepdims=True)
    inverse = 1.0 / total
    for j in range(picked + 1):
        rows = pl.ds(j * SPAN, SPAN)
        weights[rows, :] = (scores[rows, :] * inverse).astype(bf16)
    g = stack_heads(g_ref)
    out_t = lax.dot_general(values[...], weights[...], TN, preferred_element_type=f32)
    out_t = out_t.astype(bf16).astype(f32)
    store_heads(out_ref, out_t)
    delta = jnp.sum(g.astype(f32).T * out_t, axis=0, keepdims=True)
    inverse = inverse * SCALE
    for j in range(picked + 1):
        rows = pl.ds(j * SPAN, SPAN)
        part = lax.dot_general(values[rows, :], g, NT, preferred_element_type=f32)
        slopes[rows, :] = (scores[rows, :] * inverse * (part - delta)).astype(bf16)
    store_heads(dq_ref, lax.dot_general(keys[...], slopes[...], TN, preferred_element_type=f32))
    key_part = jnp.dot(slopes[...], q, preferred_element_type=f32)
    value_part = jnp.dot(weights[...], g, preferred_element_type=f32)
    ownk_ref[...] = key_part[:SPAN]
    ownv_ref[...] = value_part[:SPAN]
    for j, owner in enumerate(owners):
        step = (jnp.maximum(owner, 0) // RING - mine + lines) % lines
        rows = slice((j + 1) * SPAN, (j + 2) * SPAN)
        far = (owner % RING - at + RING) % RING
        for index, group in enumerate(GROUPS):
            inside, place = jnp.bool_(False), jnp.int32(0)
            for entry, member in enumerate(group):
                inside = inside | (far == member)
                place = jnp.where(far == member, entry, place)
            for line in range(lines):
                @pl.when((owner >= 0) & inside & (step == line))
                def _():
                    ref = sent[index * lines + line]
                    ref[place, :, :HEAD_DIM] = key_part[rows].astype(bf16)
                    ref[place, :, HEAD_DIM:] = value_part[rows].astype(bf16)


def line_sum_kernel(group, passed, me_ref, table_ref, *refs):
    refs = refs[:len(refs) - passed]
    outs = refs[-len(group):]
    lines = math.isqrt((table_ref.shape[0] - 1) // RING)
    backs = refs[-len(group) - lines:-len(group)]
    pairs = lines * RING
    me = me_ref[0]
    mine, at = me // RING, me % RING
    for entry, (far, out) in enumerate(zip(group, outs)):
        owner = (at + far) % RING
        halves = [
            table_ref[(mine - step + lines) % lines * pairs + mine * RING + owner] for step in range(lines)
        ]
        parts = [back[entry].astype(f32) for back in backs]
        for side in range(2):
            total = jnp.zeros((SPAN, 2 * HEAD_DIM), f32)
            for half, part in zip(halves, parts):
                total += jnp.where(half == side, part, 0.0)
            out[side * SPAN:(side + 1) * SPAN, :] = total.astype(bf16)


def add_kernel(ownk_ref, ownv_ref, *refs):
    parts, outs = refs[:RING], refs[RING:]
    for which, (own, out) in enumerate(zip((ownk_ref, ownv_ref), outs)):
        total = own[...]
        for part in parts:
            total += part[:, which * HEAD_DIM:(which + 1) * HEAD_DIM].astype(f32)
        out[...] = total.astype(bf16)


def body(queries, key_rows, value_rows, span_place, block_lists, cotangent):
    pairs = lax.axis_size("seq")
    lines = pairs // RING
    head_count = lax.axis_size("head")
    picked = block_lists.shape[1]
    width = queries.shape[1]
    me = lax.axis_index("seq").astype(jnp.int32)[None]
    shape = jax.ShapeDtypeStruct
    lined = shape((RING, SPAN, 2 * HEAD_DIM), bf16)
    both = shape((2 * SPAN, 2 * HEAD_DIM), bf16)

    def shift(array, y_step, z_step):
        moves = [
            (y * RING + z, (y + y_step) % lines * RING + (z + z_step) % RING)
            for y in range(lines)
            for z in range(RING)
        ]
        return lax.ppermute(array, "seq", moves)

    def over_lines(parts):
        got = list(parts)
        for step in (1, lines - 1, *range(2, lines - 1)):
            got[step] = shift(parts[step], step, 0)
        return got

    own = jnp.concatenate([key_rows, value_rows], axis=1)
    below, above = [own], [own]
    for _ in range(RING // 2 - 1):
        below.append(shift(below[-1], 0, 1))
        above.append(shift(above[-1], 0, -1))
    above.append(shift(above[-1], 0, -1))
    picks, table = pl.pallas_call(
        route_kernel,
        out_shape=(shape((2 * picked,), jnp.int32), shape((lines * pairs + 1,), jnp.int32)),
        in_specs=[SMEM, SMEM, SMEM],
        out_specs=(SMEM, SMEM),
        scratch_shapes=[pltpu.SMEM((2 * pairs,), jnp.int32)],
        compiler_params=params(),
        name="route",
    )(me, span_place, block_lists)
    lined_out = pl.pallas_call(
        line_kernel,
        out_shape=[lined] * lines,
        in_specs=[SMEM, SMEM] + [VMEM] * RING,
        out_specs=[VMEM] * lines,
        compiler_params=params(),
        name="line",
    )(me, table, *above, *below[:0:-1])
    got = over_lines(lined_out)
    columns = pl.pallas_call(
        columns_kernel,
        out_shape=shape((head_count, cotangent.shape[0], width), bf16),
        in_specs=[VMEM, ANY],
        out_specs=VMEM,
        compiler_params=params(),
        name="columns",
    )(cotangent, lined_out[0])
    grad_heads = lax.all_to_all(columns, "head", split_axis=0, concat_axis=0, tiled=True)
    grad_heads = grad_heads.reshape(queries.shape)

    rows_all = (picked + 1) * SPAN
    half_wide = pl.BlockSpec((SPAN, width), lambda i: (i, 0))
    half_head = pl.BlockSpec((SPAN, HEAD_DIM), lambda i: (i, 0))
    eighth = pl.BlockSpec(lined.shape, lambda i: (0, 0, 0))
    attended, query_grad, own_keys, own_values, *sent = pl.pallas_call(
        attend_kernel,
        grid=(2,),
        out_shape=[
            shape(queries.shape, bf16),
            shape(queries.shape, bf16),
            shape(key_rows.shape, f32),
            shape(key_rows.shape, f32),
        ] + [shape((len(group), *lined.shape[1:]), bf16) for group in GROUPS for _ in range(lines)],
        in_specs=[SMEM, SMEM, half_wide, half_wide, half_head, half_head] + [eighth] * lines,
        out_specs=[half_wide, half_wide, half_head, half_head]
        + [pl.BlockSpec((len(group), *lined.shape[1:]), lambda i: (0, 0, 0)) for group in GROUPS for _ in range(lines)],
        scratch_shapes=[
            pltpu.VMEM((lines, *lined.shape), bf16),
            pltpu.VMEM((rows_all, HEAD_DIM), bf16),
            pltpu.VMEM((rows_all, HEAD_DIM), bf16),
            pltpu.VMEM((rows_all, width), f32),
            pltpu.VMEM((rows_all, width), bf16),
            pltpu.VMEM((rows_all, width), bf16),
        ],
        compiler_params=params(),
        name="attend",
    )(me, picks, queries, grad_heads, key_rows, value_rows, *got)

    attended_out = lax.all_to_all(attended, "head", split_axis=0, concat_axis=1, tiled=True)
    back = []
    for index, group in enumerate(GROUPS):
        after = [attended_out] if index == 0 else []
        later = sent[(index + 1) * lines:]
        first = 2 + len(after)
        sums = pl.pallas_call(
            functools.partial(line_sum_kernel, group, len(later)),
            out_shape=[both] * len(group) + [shape(part.shape, bf16) for part in later],
            in_specs=[SMEM, SMEM] + [ANY] * (len(after) + len(later)) + [VMEM] * lines,
            out_specs=[VMEM] * len(group) + [ANY] * len(later),
            input_output_aliases={first + i: len(group) + i for i in range(len(later))},
            compiler_params=params(),
            name="line_sum",
        )(me, table, *after, *later, *over_lines(sent[index * lines:(index + 1) * lines]))
        sent[(index + 1) * lines:] = sums[len(group):]
        back += [shift(part, 0, far) if far else part for far, part in zip(group, sums)]
    key_grad, value_grad = pl.pallas_call(
        add_kernel,
        out_shape=(shape(key_rows.shape, bf16), shape(value_rows.shape, bf16)),
        in_specs=[VMEM] * (2 + RING),
        out_specs=(VMEM, VMEM),
        compiler_params=params(),
        name="add",
    )(own_keys, own_values, *back)
    return (attended_out, query_grad, key_grad, value_grad)


def solution(mesh):
    in_specs = (
        P("seq", "head"),
        P("seq", "head"),
        P("seq", "head"),
        P(),
        P(),
        P(("seq", "head"), None),
    )
    out_specs = (P(("seq", "head"), None), P("seq", "head"), P("seq", "head"), P("seq", "head"))
    return jax.shard_map(body, mesh=mesh, in_specs=in_specs, out_specs=out_specs, check_vma=False)
```

```python
import functools
import math

import jax
import jax.numpy as jnp
from jax import lax
from jax.experimental import pallas as pl
from jax.experimental.pallas import tpu as pltpu
from jax.sharding import PartitionSpec as P

HEAD_DIM = 128
SPAN = 128
RING = 8
HIDDEN = -1.0e30
GROUPS = ((3, 5, 4, 0), (2, 6, 1, 7))
SCALE = 1.0 / math.sqrt(HEAD_DIM)
SMEM = pl.BlockSpec(memory_space=pltpu.SMEM)
VMEM = pl.BlockSpec(memory_space=pltpu.VMEM)
ANY = pl.BlockSpec(memory_space=pl.ANY)
NT = (((1,), (1,)), ((), ()))
TN = (((0,), (0,)), ((), ()))
bf16 = jnp.bfloat16
f32 = jnp.float32


def params(mib=40):
    return pltpu.CompilerParams(vmem_limit_bytes=mib * 1024 * 1024)


def route_kernel(me_ref, place_ref, lists_ref, picks_ref, table_ref, slot_of):
    pairs = place_ref.shape[0] // 2
    picked = lists_ref.shape[1]
    lines = pairs // RING
    me = me_ref[0]
    for slot in range(2 * pairs):
        slot_of[place_ref[slot]] = slot
    for at in range(lines * pairs):
        table_ref[at] = -1
    marks = []
    for line in range(lines):
        other = line * RING + me % RING
        for side in range(2):
            block = place_ref[2 * other + side]
            for j in range(picked):
                pick = lists_ref[block, j]
                slot = slot_of[pick]
                marks.append((jnp.where(pick == block, lines * pairs, line * pairs + slot // 2), slot % 2))
    own = []
    for side in range(2):
        block = place_ref[2 * me + side]
        for j in range(picked):
            pick = lists_ref[block, j]
            own.append(jnp.where(pick == block, -1, slot_of[pick] // 2))
    for at, half in marks:
        table_ref[at] = half
    for at, owner in enumerate(own):
        picks_ref[at] = owner


def columns_kernel(cot_ref, after_ref, cols_ref):
    wide = cols_ref.shape[2]
    for part in range(cols_ref.shape[0]):
        cols_ref[part] = cot_ref[:, part * wide:(part + 1) * wide]


def line_kernel(me_ref, table_ref, *refs):
    blocks, outs = refs[:RING], refs[RING:]
    lines = len(outs)
    pairs = lines * RING
    me = me_ref[0]
    mine, at = me // RING, me % RING
    for shift, block in enumerate(blocks):
        source = (at + shift) % RING
        for step, out in enumerate(outs):
            half = table_ref[(mine + step) % lines * pairs + mine * RING + source]
            out[source] = block[pl.ds(pl.multiple_of(jnp.maximum(half, 0) * SPAN, SPAN), SPAN), :]


def stack_heads(ref):
    return jnp.concatenate(
        [ref[:, h * HEAD_DIM:(h + 1) * HEAD_DIM] for h in range(ref.shape[1] // HEAD_DIM)], axis=0
    )


def store_heads(ref, transposed):
    rows = transposed.T.astype(bf16)
    for h in range(ref.shape[1] // HEAD_DIM):
        ref[:, h * HEAD_DIM:(h + 1) * HEAD_DIM] = rows[h * SPAN:(h + 1) * SPAN, :]


def attend_kernel(me_ref, picks_ref, q_ref, g_ref, k_ref, v_ref, *refs):
    lines = (len(refs) - 10) // (1 + len(GROUPS))
    got, (out_ref, dq_ref, ownk_ref, ownv_ref), sent = refs[:lines], refs[lines:lines + 4], refs[lines + 4:-6]
    pool, keys, values, scores, weights, slopes = refs[-6:]
    slot = pl.program_id(0)
    mine, at = me_ref[0] // RING, me_ref[0] % RING
    picked = picks_ref.shape[0] // 2
    owners = [picks_ref[slot * picked + j] for j in range(picked)]

    @pl.when(slot == 0)
    def _():
        for far, ref in enumerate(got):
            pool[far] = ref[...]

    keys[:SPAN] = k_ref[...]
    values[:SPAN] = v_ref[...]
    for j, owner in enumerate(owners):
        owner = jnp.maximum(owner, 0)
        far = (mine - owner // RING + lines) % lines
        keys[(j + 1) * SPAN:(j + 2) * SPAN, :] = pool[far, owner % RING, :, :HEAD_DIM]
        values[(j + 1) * SPAN:(j + 2) * SPAN, :] = pool[far, owner % RING, :, HEAD_DIM:]
    q = stack_heads(q_ref)
    across = q.shape[0]
    top = None
    for j in range(picked + 1):
        rows = pl.ds(j * SPAN, SPAN)
        part = lax.dot_general(keys[rows, :], q, NT, preferred_element_type=f32)
        part = part * (SCALE * math.log2(math.e))
        if j == 0:
            key_at = lax.broadcasted_iota(jnp.int32, (SPAN, across), 0)
            query_at = lax.broadcasted_iota(jnp.int32, (SPAN, across), 1) % SPAN
            part = jnp.where(key_at <= query_at, part, HIDDEN)
        else:
            part = jnp.where(owners[j - 1] >= 0, part, HIDDEN)
        scores[rows, :] = part
        here = jnp.max(part, axis=0, keepdims=True)
        top = here if top is None else jnp.maximum(top, here)
    total = jnp.zeros_like(top)
    for j in range(picked + 1):
        rows = pl.ds(j * SPAN, SPAN)
        part = jnp.exp2(scores[rows, :] - top)
        scores[rows, :] = part
        total = total + jnp.sum(part, axis=0, keepdims=True)
    inverse = 1.0 / total
    for j in range(picked + 1):
        rows = pl.ds(j * SPAN, SPAN)
        weights[rows, :] = (scores[rows, :] * inverse).astype(bf16)
    g = stack_heads(g_ref)
    out_t = lax.dot_general(values[...], weights[...], TN, preferred_element_type=f32)
    out_t = out_t.astype(bf16).astype(f32)
    store_heads(out_ref, out_t)
    delta = jnp.sum(g.astype(f32).T * out_t, axis=0, keepdims=True)
    inverse = inverse * SCALE
    for j in range(picked + 1):
        rows = pl.ds(j * SPAN, SPAN)
        part = lax.dot_general(values[rows, :], g, NT, preferred_element_type=f32)
        slopes[rows, :] = (scores[rows, :] * inverse * (part - delta)).astype(bf16)
    store_heads(dq_ref, lax.dot_general(keys[...], slopes[...], TN, preferred_element_type=f32))
    key_part = jnp.dot(slopes[...], q, preferred_element_type=f32)
    value_part = jnp.dot(weights[...], g, preferred_element_type=f32)
    ownk_ref[...] = key_part[:SPAN]
    ownv_ref[...] = value_part[:SPAN]
    for j, owner in enumerate(owners):
        step = (jnp.maximum(owner, 0) // RING - mine + lines) % lines
        rows = slice((j + 1) * SPAN, (j + 2) * SPAN)
        far = (owner % RING - at + RING) % RING
        for index, group in enumerate(GROUPS):
            inside, place = jnp.bool_(False), jnp.int32(0)
            for entry, member in enumerate(group):
                inside = inside | (far == member)
                place = jnp.where(far == member, entry, place)
            for line in range(lines):
                @pl.when((owner >= 0) & inside & (step == line))
                def _():
                    ref = sent[index * lines + line]
                    ref[place, :, :HEAD_DIM] = key_part[rows].astype(bf16)
                    ref[place, :, HEAD_DIM:] = value_part[rows].astype(bf16)


def line_sum_kernel(group, me_ref, table_ref, *refs):
    outs = refs[-len(group):]
    lines = math.isqrt((table_ref.shape[0] - 1) // RING)
    backs = refs[-len(group) - lines:-len(group)]
    pairs = lines * RING
    me = me_ref[0]
    mine, at = me // RING, me % RING
    for entry, (far, out) in enumerate(zip(group, outs)):
        owner = (at + far) % RING
        halves = [
            table_ref[(mine - step + lines) % lines * pairs + mine * RING + owner] for step in range(lines)
        ]
        parts = [back[entry].astype(f32) for back in backs]
        for side in range(2):
            total = jnp.zeros((SPAN, 2 * HEAD_DIM), f32)
            for half, part in zip(halves, parts):
                total += jnp.where(half == side, part, 0.0)
            out[side * SPAN:(side + 1) * SPAN, :] = total.astype(bf16)


def hold_kernel(*refs):
    pass


def add_kernel(ownk_ref, ownv_ref, *refs):
    parts, outs = refs[:RING], refs[RING:]
    for which, (own, out) in enumerate(zip((ownk_ref, ownv_ref), outs)):
        total = own[...]
        for part in parts:
            total += part[:, which * HEAD_DIM:(which + 1) * HEAD_DIM].astype(f32)
        out[...] = total.astype(bf16)


def body(queries, key_rows, value_rows, span_place, block_lists, cotangent):
    pairs = lax.axis_size("seq")
    lines = pairs // RING
    head_count = lax.axis_size("head")
    picked = block_lists.shape[1]
    width = queries.shape[1]
    me = lax.axis_index("seq").astype(jnp.int32)[None]
    shape = jax.ShapeDtypeStruct
    lined = shape((RING, SPAN, 2 * HEAD_DIM), bf16)
    both = shape((2 * SPAN, 2 * HEAD_DIM), bf16)

    def shift(array, y_step, z_step):
        moves = [
            (y * RING + z, (y + y_step) % lines * RING + (z + z_step) % RING)
            for y in range(lines)
            for z in range(RING)
        ]
        return lax.ppermute(array, "seq", moves)

    def over_lines(parts):
        got = list(parts)
        for step in (1, lines - 1, *range(2, lines - 1)):
            got[step] = shift(parts[step], step, 0)
        return got

    own = jnp.concatenate([key_rows, value_rows], axis=1)
    below, above = [own], [own]
    for _ in range(RING // 2 - 1):
        below.append(shift(below[-1], 0, 1))
        above.append(shift(above[-1], 0, -1))
    above.append(shift(above[-1], 0, -1))
    picks, table = pl.pallas_call(
        route_kernel,
        out_shape=(shape((2 * picked,), jnp.int32), shape((lines * pairs + 1,), jnp.int32)),
        in_specs=[SMEM, SMEM, SMEM],
        out_specs=(SMEM, SMEM),
        scratch_shapes=[pltpu.SMEM((2 * pairs,), jnp.int32)],
        compiler_params=params(),
        name="route",
    )(me, span_place, block_lists)
    lined_out = pl.pallas_call(
        line_kernel,
        out_shape=[lined] * lines,
        in_specs=[SMEM, SMEM] + [VMEM] * RING,
        out_specs=[VMEM] * lines,
        compiler_params=params(),
        name="line",
    )(me, table, *above, *below[:0:-1])
    got = over_lines(lined_out)
    columns = pl.pallas_call(
        columns_kernel,
        out_shape=shape((head_count, cotangent.shape[0], width), bf16),
        in_specs=[VMEM, ANY],
        out_specs=VMEM,
        compiler_params=params(),
        name="columns",
    )(cotangent, lined_out[0])
    grad_heads = lax.all_to_all(columns, "head", split_axis=0, concat_axis=0, tiled=True)
    grad_heads = grad_heads.reshape(queries.shape)

    rows_all = (picked + 1) * SPAN
    half_wide = pl.BlockSpec((SPAN, width), lambda i: (i, 0))
    half_head = pl.BlockSpec((SPAN, HEAD_DIM), lambda i: (i, 0))
    eighth = pl.BlockSpec(lined.shape, lambda i: (0, 0, 0))
    attended, query_grad, own_keys, own_values, *sent = pl.pallas_call(
        attend_kernel,
        grid=(2,),
        out_shape=[
            shape(queries.shape, bf16),
            shape(queries.shape, bf16),
            shape(key_rows.shape, f32),
            shape(key_rows.shape, f32),
        ] + [shape((len(group), *lined.shape[1:]), bf16) for group in GROUPS for _ in range(lines)],
        in_specs=[SMEM, SMEM, half_wide, half_wide, half_head, half_head] + [eighth] * lines,
        out_specs=[half_wide, half_wide, half_head, half_head]
        + [pl.BlockSpec((len(group), *lined.shape[1:]), lambda i: (0, 0, 0)) for group in GROUPS for _ in range(lines)],
        scratch_shapes=[
            pltpu.VMEM((lines, *lined.shape), bf16),
            pltpu.VMEM((rows_all, HEAD_DIM), bf16),
            pltpu.VMEM((rows_all, HEAD_DIM), bf16),
            pltpu.VMEM((rows_all, width), f32),
            pltpu.VMEM((rows_all, width), bf16),
            pltpu.VMEM((rows_all, width), bf16),
        ],
        compiler_params=params(),
        name="attend",
    )(me, picks, queries, grad_heads, key_rows, value_rows, *got)

    attended_out = lax.all_to_all(attended, "head", split_axis=0, concat_axis=1, tiled=True)
    back = []
    later = sent[lines:]
    sent[lines:] = pl.pallas_call(
        hold_kernel,
        out_shape=[shape(part.shape, bf16) for part in later],
        in_specs=[ANY] * len(later),
        out_specs=[ANY] * len(later),
        input_output_aliases={i: i for i in range(len(later))},
        compiler_params=params(),
        cost_estimate=pl.CostEstimate(flops=5_000_000_000, bytes_accessed=0, transcendentals=0),
        name="hold",
    )(*later)
    for index, group in enumerate(GROUPS):
        sums = pl.pallas_call(
            functools.partial(line_sum_kernel, group),
            out_shape=[both] * len(group),
            in_specs=[SMEM, SMEM] + [VMEM] * lines,
            out_specs=[VMEM] * len(group),
            compiler_params=params(),
            name="line_sum",
        )(me, table, *over_lines(sent[index * lines:(index + 1) * lines]))
        back += [shift(part, 0, far) if far else part for far, part in zip(group, sums)]
    key_grad, value_grad = pl.pallas_call(
        add_kernel,
        out_shape=(shape(key_rows.shape, bf16), shape(value_rows.shape, bf16)),
        in_specs=[VMEM] * (2 + RING),
        out_specs=(VMEM, VMEM),
        compiler_params=params(),
        name="add",
    )(own_keys, own_values, *back)
    return (attended_out, query_grad, key_grad, value_grad)


def solution(mesh):
    in_specs = (
        P("seq", "head"),
        P("seq", "head"),
        P("seq", "head"),
        P(),
        P(),
        P(("seq", "head"), None),
    )
    out_specs = (P(("seq", "head"), None), P("seq", "head"), P("seq", "head"), P("seq", "head"))
    return jax.shard_map(body, mesh=mesh, in_specs=in_specs, out_specs=out_specs, check_vma=False)
```

```python
import functools
import math

import jax
import jax.numpy as jnp
from jax import lax
from jax.experimental import pallas as pl
from jax.experimental.pallas import tpu as pltpu
from jax.sharding import PartitionSpec as P

HEAD_DIM = 128
SPAN = 128
RING = 8
HIDDEN = -1.0e30
STEPS = (0, 1, 3, 2)
GROUPS = ((3, 5, 4, 0), (2, 6, 1, 7))
SCALE = 1.0 / math.sqrt(HEAD_DIM)
SMEM = pl.BlockSpec(memory_space=pltpu.SMEM)
VMEM = pl.BlockSpec(memory_space=pltpu.VMEM)
ANY = pl.BlockSpec(memory_space=pl.ANY)
NT = (((1,), (1,)), ((), ()))
TN = (((0,), (0,)), ((), ()))
bf16 = jnp.bfloat16
f32 = jnp.float32


def params(mib=40):
    return pltpu.CompilerParams(vmem_limit_bytes=mib * 1024 * 1024)


def route_kernel(me_ref, place_ref, lists_ref, picks_ref, table_ref, slot_of):
    pairs = place_ref.shape[0] // 2
    picked = lists_ref.shape[1]
    lines = pairs // RING
    me = me_ref[0]
    for slot in range(2 * pairs):
        slot_of[place_ref[slot]] = slot
    for at in range(lines * pairs):
        table_ref[at] = -1
    marks = []
    for line in range(lines):
        other = line * RING + me % RING
        for side in range(2):
            block = place_ref[2 * other + side]
            for j in range(picked):
                pick = lists_ref[block, j]
                slot = slot_of[pick]
                marks.append((jnp.where(pick == block, lines * pairs, line * pairs + slot // 2), slot % 2))
    own = []
    for side in range(2):
        block = place_ref[2 * me + side]
        for j in range(picked):
            pick = lists_ref[block, j]
            own.append(jnp.where(pick == block, -1, slot_of[pick] // 2))
    for at, half in marks:
        table_ref[at] = half
    for at, owner in enumerate(own):
        picks_ref[at] = owner


def columns_kernel(cot_ref, after_ref, cols_ref):
    wide = cols_ref.shape[2]
    for part in range(cols_ref.shape[0]):
        cols_ref[part] = cot_ref[:, part * wide:(part + 1) * wide]


def line_kernel(me_ref, table_ref, *refs):
    blocks, outs = refs[:RING], refs[RING:]
    lines = len(outs)
    pairs = lines * RING
    me = me_ref[0]
    mine, at = me // RING, me % RING
    for shift, block in enumerate(blocks):
        source = (at + shift) % RING
        for step, out in enumerate(outs):
            half = table_ref[(mine + step) % lines * pairs + mine * RING + source]
            out[source] = block[pl.ds(pl.multiple_of(jnp.maximum(half, 0) * SPAN, SPAN), SPAN), :]


def stack_heads(ref):
    return jnp.concatenate(
        [ref[:, h * HEAD_DIM:(h + 1) * HEAD_DIM] for h in range(ref.shape[1] // HEAD_DIM)], axis=0
    )


def store_heads(ref, transposed):
    rows = transposed.T.astype(bf16)
    for h in range(ref.shape[1] // HEAD_DIM):
        ref[:, h * HEAD_DIM:(h + 1) * HEAD_DIM] = rows[h * SPAN:(h + 1) * SPAN, :]


def attend_kernel(me_ref, picks_ref, q_ref, g_ref, k_ref, v_ref, *refs):
    lines = (len(refs) - 10) // (1 + len(GROUPS))
    got, (out_ref, dq_ref, ownk_ref, ownv_ref), sent = refs[:lines], refs[lines:lines + 4], refs[lines + 4:-6]
    pool, keys, values, scores, weights, slopes = refs[-6:]
    slot = pl.program_id(0)
    mine, at = me_ref[0] // RING, me_ref[0] % RING
    picked = picks_ref.shape[0] // 2
    owners = [picks_ref[slot * picked + j] for j in range(picked)]

    @pl.when(slot == 0)
    def _():
        for far, ref in zip(STEPS, got):
            pool[far] = ref[...]

    keys[:SPAN] = k_ref[...]
    values[:SPAN] = v_ref[...]
    for j, owner in enumerate(owners):
        owner = jnp.maximum(owner, 0)
        far = (mine - owner // RING + lines) % lines
        keys[(j + 1) * SPAN:(j + 2) * SPAN, :] = pool[far, owner % RING, :, :HEAD_DIM]
        values[(j + 1) * SPAN:(j + 2) * SPAN, :] = pool[far, owner % RING, :, HEAD_DIM:]
    q = stack_heads(q_ref)
    across = q.shape[0]
    top = None
    for j in range(picked + 1):
        rows = pl.ds(j * SPAN, SPAN)
        part = lax.dot_general(keys[rows, :], q, NT, preferred_element_type=f32)
        part = part * (SCALE * math.log2(math.e))
        if j == 0:
            key_at = lax.broadcasted_iota(jnp.int32, (SPAN, across), 0)
            query_at = lax.broadcasted_iota(jnp.int32, (SPAN, across), 1) % SPAN
            part = jnp.where(key_at <= query_at, part, HIDDEN)
        else:
            part = jnp.where(owners[j - 1] >= 0, part, HIDDEN)
        scores[rows, :] = part
        here = jnp.max(part, axis=0, keepdims=True)
        top = here if top is None else jnp.maximum(top, here)
    total = jnp.zeros_like(top)
    for j in range(picked + 1):
        rows = pl.ds(j * SPAN, SPAN)
        part = jnp.exp2(scores[rows, :] - top)
        scores[rows, :] = part
        total = total + jnp.sum(part, axis=0, keepdims=True)
    inverse = 1.0 / total
    for j in range(picked + 1):
        rows = pl.ds(j * SPAN, SPAN)
        weights[rows, :] = (scores[rows, :] * inverse).astype(bf16)
    g = stack_heads(g_ref)
    out_t = lax.dot_general(values[...], weights[...], TN, preferred_element_type=f32)
    out_t = out_t.astype(bf16).astype(f32)
    store_heads(out_ref, out_t)
    delta = jnp.sum(g.astype(f32).T * out_t, axis=0, keepdims=True)
    inverse = inverse * SCALE
    for j in range(picked + 1):
        rows = pl.ds(j * SPAN, SPAN)
        part = lax.dot_general(values[rows, :], g, NT, preferred_element_type=f32)
        slopes[rows, :] = (scores[rows, :] * inverse * (part - delta)).astype(bf16)
    store_heads(dq_ref, lax.dot_general(keys[...], slopes[...], TN, preferred_element_type=f32))
    key_part = jnp.dot(slopes[...], q, preferred_element_type=f32)
    value_part = jnp.dot(weights[...], g, preferred_element_type=f32)
    ownk_ref[...] = key_part[:SPAN]
    ownv_ref[...] = value_part[:SPAN]
    for j, owner in enumerate(owners):
        step = (jnp.maximum(owner, 0) // RING - mine + lines) % lines
        rows = slice((j + 1) * SPAN, (j + 2) * SPAN)
        far = (owner % RING - at + RING) % RING
        for index, group in enumerate(GROUPS):
            inside, place = jnp.bool_(False), jnp.int32(0)
            for entry, member in enumerate(group):
                inside = inside | (far == member)
                place = jnp.where(far == member, entry, place)
            for line in range(lines):
                @pl.when((owner >= 0) & inside & (step == line))
                def _():
                    ref = sent[index * lines + line]
                    ref[place, :, :HEAD_DIM] = key_part[rows].astype(bf16)
                    ref[place, :, HEAD_DIM:] = value_part[rows].astype(bf16)


def line_sum_kernel(group, me_ref, table_ref, *refs):
    outs = refs[-len(group):]
    lines = math.isqrt((table_ref.shape[0] - 1) // RING)
    backs = refs[-len(group) - lines:-len(group)]
    pairs = lines * RING
    me = me_ref[0]
    mine, at = me // RING, me % RING
    for entry, (far, out) in enumerate(zip(group, outs)):
        owner = (at + far) % RING
        halves = [
            table_ref[(mine - step + lines) % lines * pairs + mine * RING + owner] for step in STEPS
        ]
        parts = [back[entry].astype(f32) for back in backs]
        for side in range(2):
            total = jnp.zeros((SPAN, 2 * HEAD_DIM), f32)
            for half, part in zip(halves, parts):
                total += jnp.where(half == side, part, 0.0)
            out[side * SPAN:(side + 1) * SPAN, :] = total.astype(bf16)


def hold_kernel(*refs):
    pass


def add_kernel(ownk_ref, ownv_ref, *refs):
    parts, outs = refs[:RING], refs[RING:]
    for which, (own, out) in enumerate(zip((ownk_ref, ownv_ref), outs)):
        total = own[...]
        for part in parts:
            total += part[:, which * HEAD_DIM:(which + 1) * HEAD_DIM].astype(f32)
        out[...] = total.astype(bf16)


def body(queries, key_rows, value_rows, span_place, block_lists, cotangent):
    pairs = lax.axis_size("seq")
    lines = pairs // RING
    head_count = lax.axis_size("head")
    picked = block_lists.shape[1]
    width = queries.shape[1]
    me = lax.axis_index("seq").astype(jnp.int32)[None]
    shape = jax.ShapeDtypeStruct
    lined = shape((RING, SPAN, 2 * HEAD_DIM), bf16)
    both = shape((2 * SPAN, 2 * HEAD_DIM), bf16)

    def shift(array, y_step, z_step):
        moves = [
            (y * RING + z, (y + y_step) % lines * RING + (z + z_step) % RING)
            for y in range(lines)
            for z in range(RING)
        ]
        return lax.ppermute(array, "seq", moves)

    def over_lines(parts):
        return [shift(parts[step], step, 0) if step else parts[step] for step in STEPS]

    own = jnp.concatenate([key_rows, value_rows], axis=1)
    below, above = [own], [own]
    for _ in range(RING // 2 - 1):
        below.append(shift(below[-1], 0, 1))
        above.append(shift(above[-1], 0, -1))
    above.append(shift(above[-1], 0, -1))
    picks, table = pl.pallas_call(
        route_kernel,
        out_shape=(shape((2 * picked,), jnp.int32), shape((lines * pairs + 1,), jnp.int32)),
        in_specs=[SMEM, SMEM, SMEM],
        out_specs=(SMEM, SMEM),
        scratch_shapes=[pltpu.SMEM((2 * pairs,), jnp.int32)],
        compiler_params=params(),
        name="route",
    )(me, span_place, block_lists)
    lined_out = pl.pallas_call(
        line_kernel,
        out_shape=[lined] * lines,
        in_specs=[SMEM, SMEM] + [VMEM] * RING,
        out_specs=[VMEM] * lines,
        compiler_params=params(),
        name="line",
    )(me, table, *above, *below[:0:-1])
    got = over_lines(lined_out)
    columns = pl.pallas_call(
        columns_kernel,
        out_shape=shape((head_count, cotangent.shape[0], width), bf16),
        in_specs=[VMEM, ANY],
        out_specs=VMEM,
        compiler_params=params(),
        name="columns",
    )(cotangent, lined_out[0])
    grad_heads = lax.all_to_all(columns, "head", split_axis=0, concat_axis=0, tiled=True)
    grad_heads = grad_heads.reshape(queries.shape)

    rows_all = (picked + 1) * SPAN
    half_wide = pl.BlockSpec((SPAN, width), lambda i: (i, 0))
    half_head = pl.BlockSpec((SPAN, HEAD_DIM), lambda i: (i, 0))
    eighth = pl.BlockSpec(lined.shape, lambda i: (0, 0, 0))
    attended, query_grad, own_keys, own_values, *sent = pl.pallas_call(
        attend_kernel,
        grid=(2,),
        out_shape=[
            shape(queries.shape, bf16),
            shape(queries.shape, bf16),
            shape(key_rows.shape, f32),
            shape(key_rows.shape, f32),
        ] + [shape((len(group), *lined.shape[1:]), bf16) for group in GROUPS for _ in range(lines)],
        in_specs=[SMEM, SMEM, half_wide, half_wide, half_head, half_head] + [eighth] * lines,
        out_specs=[half_wide, half_wide, half_head, half_head]
        + [pl.BlockSpec((len(group), *lined.shape[1:]), lambda i: (0, 0, 0)) for group in GROUPS for _ in range(lines)],
        scratch_shapes=[
            pltpu.VMEM((lines, *lined.shape), bf16),
            pltpu.VMEM((rows_all, HEAD_DIM), bf16),
            pltpu.VMEM((rows_all, HEAD_DIM), bf16),
            pltpu.VMEM((rows_all, width), f32),
            pltpu.VMEM((rows_all, width), bf16),
            pltpu.VMEM((rows_all, width), bf16),
        ],
        compiler_params=params(),
        name="attend",
    )(me, picks, queries, grad_heads, key_rows, value_rows, *got)

    attended_out = lax.all_to_all(attended, "head", split_axis=0, concat_axis=1, tiled=True)
    back = []
    later = sent[lines:]
    sent[lines:] = pl.pallas_call(
        hold_kernel,
        out_shape=[shape(part.shape, bf16) for part in later],
        in_specs=[ANY] * len(later),
        out_specs=[ANY] * len(later),
        input_output_aliases={i: i for i in range(len(later))},
        compiler_params=params(),
        cost_estimate=pl.CostEstimate(flops=5_000_000_000, bytes_accessed=0, transcendentals=0),
        name="hold",
    )(*later)
    for index, group in enumerate(GROUPS):
        sums = pl.pallas_call(
            functools.partial(line_sum_kernel, group),
            out_shape=[both] * len(group),
            in_specs=[SMEM, SMEM] + [VMEM] * lines,
            out_specs=[VMEM] * len(group),
            compiler_params=params(),
            name="line_sum",
        )(me, table, *over_lines(sent[index * lines:(index + 1) * lines]))
        back += [shift(part, 0, far) if far else part for far, part in zip(group, sums)]
    key_grad, value_grad = pl.pallas_call(
        add_kernel,
        out_shape=(shape(key_rows.shape, bf16), shape(value_rows.shape, bf16)),
        in_specs=[VMEM] * (2 + RING),
        out_specs=(VMEM, VMEM),
        compiler_params=params(),
        name="add",
    )(own_keys, own_values, *back)
    return (attended_out, query_grad, key_grad, value_grad)


def solution(mesh):
    in_specs = (
        P("seq", "head"),
        P("seq", "head"),
        P("seq", "head"),
        P(),
        P(),
        P(("seq", "head"), None),
    )
    out_specs = (P(("seq", "head"), None), P("seq", "head"), P("seq", "head"), P("seq", "head"))
    return jax.shard_map(body, mesh=mesh, in_specs=in_specs, out_specs=out_specs, check_vma=False)
```

```python
import functools
import math

import jax
import jax.numpy as jnp
from jax import lax
from jax.experimental import pallas as pl
from jax.experimental.pallas import tpu as pltpu
from jax.sharding import PartitionSpec as P

HEAD_DIM = 128
SPAN = 128
RING = 8
HIDDEN = -1.0e30
STEPS = (0, 1, 3, 2)
GROUPS = ((3, 5, 4, 0), (1, 7, 2, 6))
SCALE = 1.0 / math.sqrt(HEAD_DIM)
SMEM = pl.BlockSpec(memory_space=pltpu.SMEM)
VMEM = pl.BlockSpec(memory_space=pltpu.VMEM)
ANY = pl.BlockSpec(memory_space=pl.ANY)
NT = (((1,), (1,)), ((), ()))
TN = (((0,), (0,)), ((), ()))
bf16 = jnp.bfloat16
f32 = jnp.float32


def params(mib=40):
    return pltpu.CompilerParams(vmem_limit_bytes=mib * 1024 * 1024)


def route_kernel(me_ref, place_ref, lists_ref, picks_ref, table_ref, slot_of):
    pairs = place_ref.shape[0] // 2
    picked = lists_ref.shape[1]
    lines = pairs // RING
    me = me_ref[0]
    for slot in range(2 * pairs):
        slot_of[place_ref[slot]] = slot
    for at in range(lines * pairs):
        table_ref[at] = -1
    marks = []
    for line in range(lines):
        other = line * RING + me % RING
        for side in range(2):
            block = place_ref[2 * other + side]
            for j in range(picked):
                pick = lists_ref[block, j]
                slot = slot_of[pick]
                marks.append((jnp.where(pick == block, lines * pairs, line * pairs + slot // 2), slot % 2))
    own = []
    for side in range(2):
        block = place_ref[2 * me + side]
        for j in range(picked):
            pick = lists_ref[block, j]
            own.append(jnp.where(pick == block, -1, slot_of[pick] // 2))
    for at, half in marks:
        table_ref[at] = half
    for at, owner in enumerate(own):
        picks_ref[at] = owner


def columns_kernel(cot_ref, after_ref, cols_ref):
    wide = cols_ref.shape[2]
    for part in range(cols_ref.shape[0]):
        cols_ref[part] = cot_ref[:, part * wide:(part + 1) * wide]


def line_kernel(me_ref, table_ref, *refs):
    blocks, outs = refs[:RING], refs[RING:]
    lines = len(outs)
    pairs = lines * RING
    me = me_ref[0]
    mine, at = me // RING, me % RING
    for shift, block in enumerate(blocks):
        source = (at + shift) % RING
        for step, out in enumerate(outs):
            half = table_ref[(mine + step) % lines * pairs + mine * RING + source]
            out[source] = block[pl.ds(pl.multiple_of(jnp.maximum(half, 0) * SPAN, SPAN), SPAN), :]


def stack_heads(ref):
    return jnp.concatenate(
        [ref[:, h * HEAD_DIM:(h + 1) * HEAD_DIM] for h in range(ref.shape[1] // HEAD_DIM)], axis=0
    )


def store_heads(ref, transposed):
    rows = transposed.T.astype(bf16)
    for h in range(ref.shape[1] // HEAD_DIM):
        ref[:, h * HEAD_DIM:(h + 1) * HEAD_DIM] = rows[h * SPAN:(h + 1) * SPAN, :]


def attend_kernel(me_ref, picks_ref, q_ref, g_ref, k_ref, v_ref, *refs):
    lines = (len(refs) - 10) // (1 + len(GROUPS))
    got, (out_ref, dq_ref, ownk_ref, ownv_ref), sent = refs[:lines], refs[lines:lines + 4], refs[lines + 4:-6]
    pool, keys, values, scores, weights, slopes = refs[-6:]
    slot = pl.program_id(0)
    mine, at = me_ref[0] // RING, me_ref[0] % RING
    picked = picks_ref.shape[0] // 2
    owners = [picks_ref[slot * picked + j] for j in range(picked)]

    @pl.when(slot == 0)
    def _():
        for far, ref in zip(STEPS, got):
            pool[far] = ref[...]

    keys[:SPAN] = k_ref[...]
    values[:SPAN] = v_ref[...]
    for j, owner in enumerate(owners):
        owner = jnp.maximum(owner, 0)
        far = (mine - owner // RING + lines) % lines
        keys[(j + 1) * SPAN:(j + 2) * SPAN, :] = pool[far, owner % RING, :, :HEAD_DIM]
        values[(j + 1) * SPAN:(j + 2) * SPAN, :] = pool[far, owner % RING, :, HEAD_DIM:]
    q = stack_heads(q_ref)
    across = q.shape[0]
    top = None
    for j in range(picked + 1):
        rows = pl.ds(j * SPAN, SPAN)
        part = lax.dot_general(keys[rows, :], q, NT, preferred_element_type=f32)
        part = part * (SCALE * math.log2(math.e))
        if j == 0:
            key_at = lax.broadcasted_iota(jnp.int32, (SPAN, across), 0)
            query_at = lax.broadcasted_iota(jnp.int32, (SPAN, across), 1) % SPAN
            part = jnp.where(key_at <= query_at, part, HIDDEN)
        else:
            part = jnp.where(owners[j - 1] >= 0, part, HIDDEN)
        scores[rows, :] = part
        here = jnp.max(part, axis=0, keepdims=True)
        top = here if top is None else jnp.maximum(top, here)
    total = jnp.zeros_like(top)
    for j in range(picked + 1):
        rows = pl.ds(j * SPAN, SPAN)
        part = jnp.exp2(scores[rows, :] - top)
        scores[rows, :] = part
        total = total + jnp.sum(part, axis=0, keepdims=True)
    inverse = 1.0 / total
    for j in range(picked + 1):
        rows = pl.ds(j * SPAN, SPAN)
        weights[rows, :] = (scores[rows, :] * inverse).astype(bf16)
    g = stack_heads(g_ref)
    out_t = lax.dot_general(values[...], weights[...], TN, preferred_element_type=f32)
    out_t = out_t.astype(bf16).astype(f32)
    store_heads(out_ref, out_t)
    delta = jnp.sum(g.astype(f32).T * out_t, axis=0, keepdims=True)
    inverse = inverse * SCALE
    for j in range(picked + 1):
        rows = pl.ds(j * SPAN, SPAN)
        part = lax.dot_general(values[rows, :], g, NT, preferred_element_type=f32)
        slopes[rows, :] = (scores[rows, :] * inverse * (part - delta)).astype(bf16)
    store_heads(dq_ref, lax.dot_general(keys[...], slopes[...], TN, preferred_element_type=f32))
    key_part = jnp.dot(slopes[...], q, preferred_element_type=f32)
    value_part = jnp.dot(weights[...], g, preferred_element_type=f32)
    ownk_ref[...] = key_part[:SPAN]
    ownv_ref[...] = value_part[:SPAN]
    for j, owner in enumerate(owners):
        step = (jnp.maximum(owner, 0) // RING - mine + lines) % lines
        rows = slice((j + 1) * SPAN, (j + 2) * SPAN)
        far = (owner % RING - at + RING) % RING
        for index, group in enumerate(GROUPS):
            inside, place = jnp.bool_(False), jnp.int32(0)
            for entry, member in enumerate(group):
                inside = inside | (far == member)
                place = jnp.where(far == member, entry, place)
            for line in range(lines):
                @pl.when((owner >= 0) & inside & (step == line))
                def _():
                    ref = sent[index * lines + line]
                    ref[place, :, :HEAD_DIM] = key_part[rows].astype(bf16)
                    ref[place, :, HEAD_DIM:] = value_part[rows].astype(bf16)


def line_sum_kernel(group, me_ref, table_ref, *refs):
    outs = refs[-len(group):]
    lines = math.isqrt((table_ref.shape[0] - 1) // RING)
    backs = refs[-len(group) - lines:-len(group)]
    pairs = lines * RING
    me = me_ref[0]
    mine, at = me // RING, me % RING
    for entry, (far, out) in enumerate(zip(group, outs)):
        owner = (at + far) % RING
        halves = [
            table_ref[(mine - step + lines) % lines * pairs + mine * RING + owner] for step in STEPS
        ]
        parts = [back[entry].astype(f32) for back in backs]
        for side in range(2):
            total = jnp.zeros((SPAN, 2 * HEAD_DIM), f32)
            for half, part in zip(halves, parts):
                total += jnp.where(half == side, part, 0.0)
            out[side * SPAN:(side + 1) * SPAN, :] = total.astype(bf16)


def hold_kernel(*refs):
    pass


def add_kernel(ownk_ref, ownv_ref, *refs):
    parts, outs = refs[:RING], refs[RING:]
    for which, (own, out) in enumerate(zip((ownk_ref, ownv_ref), outs)):
        total = own[...]
        for part in parts:
            total += part[:, which * HEAD_DIM:(which + 1) * HEAD_DIM].astype(f32)
        out[...] = total.astype(bf16)


def body(queries, key_rows, value_rows, span_place, block_lists, cotangent):
    pairs = lax.axis_size("seq")
    lines = pairs // RING
    head_count = lax.axis_size("head")
    picked = block_lists.shape[1]
    width = queries.shape[1]
    me = lax.axis_index("seq").astype(jnp.int32)[None]
    shape = jax.ShapeDtypeStruct
    lined = shape((RING, SPAN, 2 * HEAD_DIM), bf16)
    both = shape((2 * SPAN, 2 * HEAD_DIM), bf16)

    def shift(array, y_step, z_step):
        moves = [
            (y * RING + z, (y + y_step) % lines * RING + (z + z_step) % RING)
            for y in range(lines)
            for z in range(RING)
        ]
        return lax.ppermute(array, "seq", moves)

    def over_lines(parts):
        return [shift(parts[step], step, 0) if step else parts[step] for step in STEPS]

    own = jnp.concatenate([key_rows, value_rows], axis=1)
    below, above = [own], [own]
    for _ in range(RING // 2 - 1):
        below.append(shift(below[-1], 0, 1))
        above.append(shift(above[-1], 0, -1))
    above.append(shift(above[-1], 0, -1))
    picks, table = pl.pallas_call(
        route_kernel,
        out_shape=(shape((2 * picked,), jnp.int32), shape((lines * pairs + 1,), jnp.int32)),
        in_specs=[SMEM, SMEM, SMEM],
        out_specs=(SMEM, SMEM),
        scratch_shapes=[pltpu.SMEM((2 * pairs,), jnp.int32)],
        compiler_params=params(),
        name="route",
    )(me, span_place, block_lists)
    lined_out = pl.pallas_call(
        line_kernel,
        out_shape=[lined] * lines,
        in_specs=[SMEM, SMEM] + [VMEM] * RING,
        out_specs=[VMEM] * lines,
        compiler_params=params(),
        name="line",
    )(me, table, *above, *below[:0:-1])
    got = over_lines(lined_out)
    columns = pl.pallas_call(
        columns_kernel,
        out_shape=shape((head_count, cotangent.shape[0], width), bf16),
        in_specs=[VMEM, ANY],
        out_specs=VMEM,
        compiler_params=params(),
        name="columns",
    )(cotangent, lined_out[0])
    grad_heads = lax.all_to_all(columns, "head", split_axis=0, concat_axis=0, tiled=True)
    grad_heads = grad_heads.reshape(queries.shape)

    rows_all = (picked + 1) * SPAN
    half_wide = pl.BlockSpec((SPAN, width), lambda i: (i, 0))
    half_head = pl.BlockSpec((SPAN, HEAD_DIM), lambda i: (i, 0))
    eighth = pl.BlockSpec(lined.shape, lambda i: (0, 0, 0))
    attended, query_grad, own_keys, own_values, *sent = pl.pallas_call(
        attend_kernel,
        grid=(2,),
        out_shape=[
            shape(queries.shape, bf16),
            shape(queries.shape, bf16),
            shape(key_rows.shape, f32),
            shape(key_rows.shape, f32),
        ] + [shape((len(group), *lined.shape[1:]), bf16) for group in GROUPS for _ in range(lines)],
        in_specs=[SMEM, SMEM, half_wide, half_wide, half_head, half_head] + [eighth] * lines,
        out_specs=[half_wide, half_wide, half_head, half_head]
        + [pl.BlockSpec((len(group), *lined.shape[1:]), lambda i: (0, 0, 0)) for group in GROUPS for _ in range(lines)],
        scratch_shapes=[
            pltpu.VMEM((lines, *lined.shape), bf16),
            pltpu.VMEM((rows_all, HEAD_DIM), bf16),
            pltpu.VMEM((rows_all, HEAD_DIM), bf16),
            pltpu.VMEM((rows_all, width), f32),
            pltpu.VMEM((rows_all, width), bf16),
            pltpu.VMEM((rows_all, width), bf16),
        ],
        compiler_params=params(),
        name="attend",
    )(me, picks, queries, grad_heads, key_rows, value_rows, *got)

    attended_out = lax.all_to_all(attended, "head", split_axis=0, concat_axis=1, tiled=True)
    back = []
    later = sent[lines:]
    sent[lines:] = pl.pallas_call(
        hold_kernel,
        out_shape=[shape(part.shape, bf16) for part in later],
        in_specs=[ANY] * len(later),
        out_specs=[ANY] * len(later),
        input_output_aliases={i: i for i in range(len(later))},
        compiler_params=params(),
        cost_estimate=pl.CostEstimate(flops=5_000_000_000, bytes_accessed=0, transcendentals=0),
        name="hold",
    )(*later)
    for index, group in enumerate(GROUPS):
        sums = pl.pallas_call(
            functools.partial(line_sum_kernel, group),
            out_shape=[both] * len(group),
            in_specs=[SMEM, SMEM] + [VMEM] * lines,
            out_specs=[VMEM] * len(group),
            compiler_params=params(),
            name="line_sum",
        )(me, table, *over_lines(sent[index * lines:(index + 1) * lines]))
        back += [shift(part, 0, far) if far else part for far, part in zip(group, sums)]
    key_grad, value_grad = pl.pallas_call(
        add_kernel,
        out_shape=(shape(key_rows.shape, bf16), shape(value_rows.shape, bf16)),
        in_specs=[VMEM] * (2 + RING),
        out_specs=(VMEM, VMEM),
        compiler_params=params(),
        name="add",
    )(own_keys, own_values, *back)
    return (attended_out, query_grad, key_grad, value_grad)


def solution(mesh):
    in_specs = (
        P("seq", "head"),
        P("seq", "head"),
        P("seq", "head"),
        P(),
        P(),
        P(("seq", "head"), None),
    )
    out_specs = (P(("seq", "head"), None), P("seq", "head"), P("seq", "head"), P("seq", "head"))
    return jax.shard_map(body, mesh=mesh, in_specs=in_specs, out_specs=out_specs, check_vma=False)
```
